32 devices in a mesh: row: 4 (over y, core), col: 8 (over z, x).
Axes of the slice: x: 2, y: 2, z: 4, core: 2. Of those that a mesh axis runs over, the one named last changes fastest.
Arguments:
- matrix: float32 [2048, 2048], P('row', 'col'), may hold values from -1 to 4, as said below
Outputs:
- reduced: float32 [2048, 2048], P('row', 'col')
The draws below stay inside these ranges and needn't reach their ends.
Inputs may be any that keep to these rules, and one draw needn't show every extreme that they name: matrix is symmetric; its diagonal entries lie between 1 and 3 up to entries of size about 2048^-1/2 that every entry carries; entries at distance 256 from the diagonal with the smaller index under 2 * 256 carry an added 2.
All inputs are finite; a program needn't handle non-finite values.
Results may differ from the reference program's by a relative error of at most 0.00019.
Values sent between devices are 32-bit elements; how exact they have to be, the bound alone decides.
A program may use at most 64 MiB of HBM per device.

```python
import math
import jax
import jax.numpy as jnp
from jax import lax

B = 256
PANELS = 1
N = 2048


def draw_matrix(key, part):
    first_key = jax.random.fold_in(key, 11)
    second_key = jax.random.fold_in(key, 23)
    noise = jax.random.normal(first_key, (N, N), jnp.float32)
    noise = (noise + noise.T) * (0.7071 / math.sqrt(N))
    diagonal = jax.random.uniform(second_key, (N,), jnp.float32, 1.0, 3.0)
    all_rows = jnp.arange(N, dtype=jnp.int32)
    apart = jnp.abs(all_rows[:, None] - all_rows[None, :]) == B
    early = jnp.minimum(all_rows[:, None], all_rows[None, :]) < 2 * B
    banded = jnp.where(apart & early, 2.0, 0.0)
    return noise + jnp.diag(diagonal) + banded


def setup_inputs(seed: int = 0) -> dict:
    keys = jax.random.split(jax.random.key(seed), 2)
    return {
        "matrix": draw_matrix(jax.random.fold_in(keys[1], 71), 0),
    }


def product(left, right):
    return jnp.dot(left.astype(jnp.float32), right.astype(jnp.float32), precision=lax.Precision.HIGHEST, preferred_element_type=jnp.float32)

def left_product(left, right):
    return lax.dot_general(left.astype(jnp.float32), right.astype(jnp.float32), (((0,), (0,)), ((), ())), precision=lax.Precision.HIGHEST, preferred_element_type=jnp.float32)

def right_product(left, right):
    return lax.dot_general(left.astype(jnp.float32), right.astype(jnp.float32), (((1,), (1,)), ((), ())), precision=lax.Precision.HIGHEST, preferred_element_type=jnp.float32)

def factor_inverse(kmat):
    cholesky_low = jnp.linalg.cholesky(left_product(kmat, kmat))
    halfway = lax.linalg.triangular_solve(cholesky_low, kmat.T, left_side=True, lower=True)
    return lax.linalg.triangular_solve(cholesky_low, halfway, left_side=True, lower=True, transpose_a=True)

def reference(matrix):
    current = matrix
    all_rows = jnp.arange(N, dtype=jnp.int32)
    columns = jnp.arange(B, dtype=jnp.int32)
    identity = jnp.eye(B, dtype=jnp.float32)
    for panel_index in range(PANELS):
        start_row = (panel_index + 1) * B
        sign = 1.0 if panel_index % 2 == 0 else -1.0
        panel = current[:, panel_index * B:(panel_index + 1) * B]
        panel = jnp.where((all_rows >= start_row)[:, None], panel, 0.0)
        top = panel[start_row:start_row + B]
        gram = left_product(panel, panel)
        cholesky_low = jnp.linalg.cholesky(gram)
        ortho = lax.linalg.triangular_solve(cholesky_low, panel, left_side=False, lower=True, transpose_a=True)
        top_q = lax.linalg.triangular_solve(cholesky_low, top, left_side=False, lower=True, transpose_a=True)
        tfac = factor_inverse(identity + sign * top_q)
        unit = (all_rows[:, None] - start_row == columns[None, :]).astype(jnp.float32)
        refl = ortho + sign * unit
        x_all = product(current, refl)
        y_full = left_product(refl, x_all)
        middle = product(product(tfac.T, y_full), tfac)
        w_all = product(x_all, tfac) - 0.5 * product(refl, middle)
        current = current - right_product(w_all, refl) - right_product(refl, w_all)
    return current
```

```python
import functools

import jax
import jax.numpy as jnp
from jax import lax
from jax.experimental import pallas as pl
from jax.experimental.pallas import tpu as pltpu
from jax.sharding import PartitionSpec as P

MESH = pl.DeviceIdType.MESH
F32 = jnp.float32


def mm(left, right, dims=((1,), (0,))):
    return lax.dot_general(
        left, right, (dims, ((), ())), precision=lax.Precision.HIGHEST, preferred_element_type=F32
    )


NT = ((1,), (1,))
TN = ((0,), (0,))


def gather_kernel(nr, nc, a_ref, pf, pi, zi, zj, gram, first, hmat, *scratch):
    (part, half_in, half_sum, half_y, red_send, red_recv, pf_send, pf_recv, ch_send, ch_recv,
     ln_send, ln_recv, top_send, top_recv) = scratch
    rows, width = a_ref.shape
    ratio = rows // width
    half = width // 2
    ny = nr // 2
    i = lax.axis_index("row")
    j = lax.axis_index("col")
    lane = lax.rem(j, ratio)
    pos = j // ratio
    core = lax.rem(i, 2)
    yy = i // 2
    base = pos * ratio

    barrier = pltpu.get_barrier_semaphore()
    for d in range(1, nr):
        pl.semaphore_signal(barrier, 1, device_id=(lax.rem(i + d, nr), j), device_id_type=MESH)
    for d in range(1, ratio):
        pl.semaphore_signal(
            barrier, 1, device_id=(i, base + lax.rem(lane + d, ratio)), device_id_type=MESH
        )

    @pl.when(pos > 0)
    def _():
        pl.semaphore_signal(barrier, 1, device_id=(i, j - ratio), device_id_type=MESH)

    @pl.when(pos < nr - 1)
    def _():
        pl.semaphore_signal(barrier, 1, device_id=(i, j + ratio), device_id_type=MESH)

    pl.semaphore_wait(
        barrier,
        nr - 1 + ratio - 1 + jnp.where(pos > 0, 1, 0) + jnp.where(pos < nr - 1, 1, 0),
    )

    def remote(src, dst, send, recv, who):
        return pltpu.make_async_remote_copy(
            src_ref=src, dst_ref=dst, send_sem=send, recv_sem=recv, device_id=who,
            device_id_type=MESH,
        )

    def column_copies(ref, sends, recvs):
        return (
            remote(ref, ref, sends.at[0], recvs, (jnp.minimum(i + 1, nr - 1), j)),
            remote(ref, ref, sends.at[1], recvs, (jnp.minimum(i + 2, nr - 1), j)),
        )

    def column_arrive(ref, sends, recvs):
        to_odd, to_even = column_copies(ref, sends, recvs)

        @pl.when(i > 0)
        def _():
            to_odd.wait_recv()

    def column_send(ref, sends, recvs):
        to_odd, to_even = column_copies(ref, sends, recvs)

        @pl.when(core == 0)
        def _():
            @pl.when(yy < ny - 1)
            def _():
                to_even.start()

            to_odd.start()

    def column_end(ref, sends, recvs):
        to_odd, to_even = column_copies(ref, sends, recvs)

        @pl.when(core == 0)
        def _():
            @pl.when(yy < ny - 1)
            def _():
                to_even.wait_send()

            to_odd.wait_send()

    def chain_copies(ref, k):
        mine = ref.at[lane]
        return (
            remote(mine, mine, ch_send.at[k, 0], ch_recv.at[k], (i, jnp.maximum(j - ratio, 0))),
            remote(mine, mine, ch_send.at[k, 1], ch_recv.at[k], (i, jnp.minimum(j + ratio, nc - 1))),
        )

    def lane_copies(ref, k):
        mine = ref.at[lane]
        out = []
        for d in range(1, ratio):
            out.append(
                remote(mine, mine, ln_send.at[k, d - 1], ln_recv.at[k, d - 1],
                       (i, base + lax.rem(lane + d, ratio)))
            )
        return out

    def chain_pass(ref, k):
        down, up = chain_copies(ref, k)

        @pl.when(pos != i)
        def _():
            down.wait_recv()

        @pl.when((pos <= i) & (pos > 0))
        def _():
            down.start()

        @pl.when((pos >= i) & (pos < nr - 1))
        def _():
            up.start()

        for c in lane_copies(ref, k):
            c.start()

    def lane_arrive(ref, k):
        for d in range(1, ratio):
            other = ref.at[lax.rem(lane - d + ratio, ratio)]
            remote(other, other, ln_send.at[k, d - 1], ln_recv.at[k, d - 1], (i, j)).wait_recv()

    def chain_end(ref, k):
        down, up = chain_copies(ref, k)

        @pl.when((pos <= i) & (pos > 0))
        def _():
            down.wait_send()

        @pl.when((pos >= i) & (pos < nr - 1))
        def _():
            up.wait_send()

        for c in lane_copies(ref, k):
            c.wait_send()

    partner = (i + 1 - 2 * core, j)
    mine_half = pl.ds(pl.multiple_of(core * half, half), half)
    other_half = pl.ds(pl.multiple_of((1 - core) * half, half), half)

    def reduce_a(k):
        return remote(part.at[k, other_half], half_in.at[k], red_send.at[k, 0], red_recv.at[k, 0], partner)

    def reduce_b(k):
        out = []
        for d in range(1, ny):
            to = lax.rem(yy + d, ny) * 2 + core
            out.append(
                remote(half_sum.at[k], half_y.at[k, yy], red_send.at[k, 1 + d],
                       red_recv.at[k, 1 + d], (to, j))
            )
        return out

    def reduce_c(k, out):
        return remote(out.at[mine_half], out.at[mine_half], red_send.at[k, 1], red_recv.at[k, 1], partner)

    def reduce_1(k):
        reduce_a(k).start()

    def reduce_2(k):
        reduce_a(k).wait_recv()
        half_sum[k] = part[k, mine_half] + half_in[k]
        for c in reduce_b(k):
            c.start()

    def reduce_3(k, out):
        for d in range(1, ny):
            slot = half_y.at[k, lax.rem(yy - d + ny, ny)]
            remote(slot, slot, red_send.at[k, 1 + d], red_recv.at[k, 1 + d], (i, j)).wait_recv()
        total = None
        for y in range(ny):
            term = jnp.where(yy == y, half_sum[k], half_y[k, y])
            total = term if total is None else total + term
        out[mine_half] = total
        reduce_c(k, out).start()

    def reduce_4(k, out):
        arrived = out.at[other_half]
        remote(arrived, arrived, red_send.at[k, 1], red_recv.at[k, 1], partner).wait_recv()

    def reduce_end(k, out):
        reduce_a(k).wait_send()
        for c in reduce_b(k):
            c.wait_send()
        reduce_c(k, out).wait_send()

    @pl.when(i == 0)
    def _():
        pf[0] = a_ref[:width] * jnp.where(j == 0, 0.0, 1.0)
        pf[1] = a_ref[width:2 * width]

    for y in range(ny):
        @pl.when(yy == y)
        def _():
            for k in range(3):
                half_y[k, y] = jnp.zeros((half, width), F32)

    for k in range(2):
        column_arrive(pf.at[k], pf_send.at[k], pf_recv.at[k])
        column_send(pf.at[k], pf_send.at[k], pf_recv.at[k])

        @pl.when(pos == i)
        def _():
            pi[k, lane] = pf[k]

        chain_pass(pi.at[k], k)

    lane_arrive(pi.at[0], 0)

    @pl.when(i == 0)
    def _():
        first[0] = pi[0, 1]
        column_send(first.at[0], top_send.at[0], top_recv.at[0])

    total = None
    for b in range(ratio):
        term = mm(pi[0, b], pi[0, b], NT)
        total = term if total is None else total + term
    part[0] = total
    reduce_1(0)
    total = None
    for b in range(ratio):
        term = mm(pi[0, b], a_ref[b * width:(b + 1) * width])
        total = term if total is None else total + term
    part[1] = total
    reduce_1(1)
    reduce_2(0)
    reduce_2(1)
    reduce_3(0, gram)
    reduce_3(1, zj)
    reduce_4(1, zj)

    @pl.when(pos == i)
    def _():
        zi[lane] = zj[...]

    chain_pass(zi, 2)
    column_arrive(first.at[0], top_send.at[0], top_recv.at[0])

    @pl.when(i > 0)
    def _():
        column_send(first.at[0], top_send.at[0], top_recv.at[0])

    lane_arrive(pi.at[1], 1)

    @pl.when(i == 0)
    def _():
        first[1] = pi[1, 1]

    column_arrive(first.at[1], top_send.at[1], top_recv.at[1])
    column_send(first.at[1], top_send.at[1], top_recv.at[1])
    lane_arrive(zi, 2)

    @pl.when(i == 0)
    def _():
        first[2] = zi[1]

    column_arrive(first.at[2], top_send.at[2], top_recv.at[2])
    column_send(first.at[2], top_send.at[2], top_recv.at[2])
    total = None
    for b in range(ratio):
        term = mm(pi[0, b], zi[b], NT)
        total = term if total is None else total + term
    part[2] = total
    reduce_1(2)
    reduce_2(2)
    reduce_3(2, hmat)
    reduce_4(2, hmat)
    reduce_4(0, gram)
    for k, out in enumerate((gram, zj, hmat)):
        reduce_end(k, out)
    for k in range(2):
        column_end(pf.at[k], pf_send.at[k], pf_recv.at[k])
        chain_end(pi.at[k], k)
    chain_end(zi, 2)
    for k in range(3):
        column_end(first.at[k], top_send.at[k], top_recv.at[k])


def small_factor(block):
    size = block.shape[0]
    step = 8
    eye = jnp.where(
        lax.broadcasted_iota(jnp.int32, (size, size), 0) == lax.broadcasted_iota(jnp.int32, (size, size), 1),
        1.0, 0.0)
    act = jnp.concatenate([block, eye], axis=1)
    lanes = 2 * size
    done = []
    for q in range(size // step):
        count = size - q * step
        rows_id = lax.broadcasted_iota(jnp.int32, (count, lanes), 0)
        cols = [
            jnp.broadcast_to(act[:, q * step + t:q * step + t + 1], (count, lanes)) for t in range(step)
        ]
        top = act[:step]
        pivots = jnp.zeros((step, lanes), F32)
        saved = []
        for t in range(step):
            pivot = cols[t][t:t + 1]
            inv = 1.0 / pivot
            mult = jnp.where(rows_id > t, cols[t], 0.0) * inv
            for u in range(t + 1, step):
                cols[u] = cols[u] - mult * cols[u][t:t + 1]
            row = top[t:t + 1]
            top = top - mult[:step] * row
            pivots = jnp.where(rows_id[:step] == t, pivot, pivots)
            saved.append((mult, row))
        done.append(top / jnp.sqrt(pivots))
        if count > step:
            rest = act[step:]
            for mult, row in saved:
                rest = rest - mult[step:] * row
            act = rest
    return jnp.concatenate(done, axis=0)[:, size:]


def update_kernel(place, a_ref, pf, pi, zi, zj, gram, first, hmat, out_ref, aug, low):
    rows, width = a_ref.shape
    ratio = rows // width
    block = 64
    i = place[0]
    j = place[1]
    one = jnp.where(
        lax.broadcasted_iota(jnp.int32, (width, width), 0)
        == lax.broadcasted_iota(jnp.int32, (width, width), 1), 1.0, 0.0)
    aug[:, :width] = gram[...]
    aug[:, width:] = one
    for q in range(width // block):
        here = slice(q * block, (q + 1) * block)
        inv = small_factor(aug[here, here])
        line = mm(inv, aug[here, :])
        low[here, :] = line[:, width:]
        if (q + 1) * block < width:
            below = slice((q + 1) * block, width)
            aug[below, :] = aug[below, :] - mm(line[:, below], line, TN)
    w = low[...]
    err = 0.5 * (one - mm(w, first[0]))

    def more(state):
        k, acc, e = state
        return (k < 40) & (jnp.max(jnp.abs(e)) > 1e-10)

    def body(state):
        k, acc, e = state
        return k + 1, acc + mm(acc, e), mm(e, e)

    _, acc, _ = lax.while_loop(more, body, (0, one + err, mm(err, err)))
    tt = 0.5 * acc
    aug[:, :width] = mm(w, first[2])
    wz = aug[:, :width]
    y = mm(mm(w, hmat[...]), w, NT) + wz + wz.T + first[1]
    half_mid = 0.5 * mm(mm(tt, y), tt, NT)

    def sides(p, f, z, is_unit):
        r = mm(w, p) + jnp.where(is_unit, one, 0.0)
        x = mm(w, z) + f
        return r, mm(tt, x) - mm(half_mid, r)

    r_cols, w_cols = sides(pf[0], pf[1], zj[...], j == 1)
    for b in range(ratio):
        r_rows, w_rows = sides(pi[0, b], pi[1, b], zi[b], i * ratio + b == 1)
        here = slice(b * width, (b + 1) * width)
        out_ref[here] = a_ref[here] - mm(w_rows, r_cols, TN) - mm(r_rows, w_cols, TN)


def solution(mesh):
    nr, nc = mesh.shape["row"], mesh.shape["col"]

    def step(matrix):
        rows, width = matrix.shape
        ratio = rows // width
        ny = nr // 2
        half = width // 2
        square = (width, width)
        vmem = pl.BlockSpec(memory_space=pltpu.VMEM)
        shapes = [(2,) + square, (2, ratio) + square, (ratio,) + square, square, square, (3,) + square, square]
        dma = pltpu.SemaphoreType.DMA
        parts = pl.pallas_call(
            functools.partial(gather_kernel, nr, nc),
            out_shape=[jax.ShapeDtypeStruct(s, F32) for s in shapes],
            in_specs=[vmem],
            out_specs=[vmem] * len(shapes),
            scratch_shapes=[
                pltpu.VMEM((3,) + square, F32),
                pltpu.VMEM((3, half, width), F32),
                pltpu.VMEM((3, half, width), F32),
                pltpu.VMEM((3, ny, half, width), F32),
                dma((3, ny + 1)), dma((3, ny + 1)),
                dma((2, 2)), dma((2,)),
                dma((3, 2)), dma((3,)),
                dma((3, ratio - 1)), dma((3, ratio - 1)),
                dma((3, 2)), dma((3,)),
            ],
            compiler_params=pltpu.CompilerParams(
                collective_id=0, has_side_effects=True, vmem_limit_bytes=48 * 2**20
            ),
            name="gather",
        )(matrix)
        return pl.pallas_call(
            update_kernel,
            out_shape=jax.ShapeDtypeStruct(matrix.shape, F32),
            in_specs=[pl.BlockSpec(memory_space=pltpu.SMEM)] + [vmem] * 8,
            out_specs=vmem,
            scratch_shapes=[pltpu.VMEM((width, 2 * width), F32), pltpu.VMEM(square, F32)],
            compiler_params=pltpu.CompilerParams(vmem_limit_bytes=48 * 2**20),
            name="update",
        )(jnp.stack([lax.axis_index("row"), lax.axis_index("col")]), matrix, *parts)

    return jax.shard_map(
        step, mesh=mesh, in_specs=(P("row", "col"),), out_specs=P("row", "col"), check_vma=False
    )
```

```python
import functools

import jax
import jax.numpy as jnp
from jax import lax
from jax.experimental import pallas as pl
from jax.experimental.pallas import tpu as pltpu
from jax.sharding import PartitionSpec as P

MESH = pl.DeviceIdType.MESH
F32 = jnp.float32
CHUNKS = 4
BLOCK = 64


def mm(left, right, dims=((1,), (0,))):
    return lax.dot_general(
        left, right, (dims, ((), ())), precision=lax.Precision.HIGHEST, preferred_element_type=F32
    )


NT = ((1,), (1,))
TN = ((0,), (0,))


def unit(size):
    same = lax.broadcasted_iota(jnp.int32, (size, size), 0) == lax.broadcasted_iota(jnp.int32, (size, size), 1)
    return jnp.where(same, 1.0, 0.0)


def gather_kernel(nr, nc, a_ref, pf, zj, low, first, ri, xi, ymat, *scratch):
    (pi, zi, gram, aug, part, half_in, half_sum, half_y, red_send, red_recv, pf_send, pf_recv, ch_send, ch_recv,
     ln_send, ln_recv, top_send, top_recv) = scratch
    rows, width = a_ref.shape
    ratio = rows // width
    half = width // 2
    ny = nr // 2
    i = lax.axis_index("row")
    j = lax.axis_index("col")
    lane = lax.rem(j, ratio)
    pos = j // ratio
    core = lax.rem(i, 2)
    yy = i // 2
    base = pos * ratio

    barrier = pltpu.get_barrier_semaphore()
    for d in range(1, nr):
        pl.semaphore_signal(barrier, 1, device_id=(lax.rem(i + d, nr), j), device_id_type=MESH)
    for d in range(1, ratio):
        pl.semaphore_signal(
            barrier, 1, device_id=(i, base + lax.rem(lane + d, ratio)), device_id_type=MESH
        )

    @pl.when(pos > 0)
    def _():
        pl.semaphore_signal(barrier, 1, device_id=(i, j - ratio), device_id_type=MESH)

    @pl.when(pos < nr - 1)
    def _():
        pl.semaphore_signal(barrier, 1, device_id=(i, j + ratio), device_id_type=MESH)

    pl.semaphore_wait(
        barrier,
        nr - 1 + ratio - 1 + jnp.where(pos > 0, 1, 0) + jnp.where(pos < nr - 1, 1, 0),
    )

    def remote(src, dst, send, recv, who):
        return pltpu.make_async_remote_copy(
            src_ref=src, dst_ref=dst, send_sem=send, recv_sem=recv, device_id=who,
            device_id_type=MESH,
        )

    chunk = width // CHUNKS
    spans = [pl.ds(c * chunk, chunk) for c in range(CHUNKS)]
    away = jnp.abs(pos - i)

    def column_copies(ref, sends, recv):
        return (
            remote(ref, ref, sends.at[0], recv, (jnp.minimum(i + 1, nr - 1), j)),
            remote(ref, ref, sends.at[1], recv, (jnp.minimum(i + 2, nr - 1), j)),
        )

    def column_arrive(ref, sends, recv):
        @pl.when(i > 0)
        def _():
            column_copies(ref, sends, recv)[0].wait_recv()

    def column_send(ref, sends, recv):
        @pl.when(core == 0)
        def _():
            to_odd, to_even = column_copies(ref, sends, recv)

            @pl.when(yy < ny - 1)
            def _():
                to_even.start()

            to_odd.start()

    def column_end(ref, sends, recv):
        @pl.when(core == 0)
        def _():
            to_odd, to_even = column_copies(ref, sends, recv)

            @pl.when(yy < ny - 1)
            def _():
                to_even.wait_send()

            to_odd.wait_send()

    def chain_copies(ref, k, c):
        mine = ref.at[lane, spans[c]]
        return (
            remote(mine, mine, ch_send.at[k, c, 0], ch_recv.at[k, c], (i, jnp.maximum(j - ratio, 0))),
            remote(mine, mine, ch_send.at[k, c, 1], ch_recv.at[k, c], (i, jnp.minimum(j + ratio, nc - 1))),
        )

    def lane_copies(ref, k, c):
        mine = ref.at[lane, spans[c]]
        return [
            remote(mine, mine, ln_send.at[k, c, d - 1], ln_recv.at[k, c, d - 1],
                   (i, base + lax.rem(lane + d, ratio)))
            for d in range(1, ratio)
        ]

    def chain_push(ref, k, c):
        down, up = chain_copies(ref, k, c)

        @pl.when((pos <= i) & (pos > 0))
        def _():
            down.start()

        @pl.when((pos >= i) & (pos < nr - 1))
        def _():
            up.start()

        for copy in lane_copies(ref, k, c):
            copy.start()

    def chain_source(ref, k, c, block):
        @pl.when(away == 0)
        def _():
            ref[lane, spans[c]] = block[spans[c]]
            chain_push(ref, k, c)

    def chain_pass(ref, k, c, far):
        @pl.when(far)
        def _():
            chain_copies(ref, k, c)[0].wait_recv()
            chain_push(ref, k, c)

    def chain_point(ref, k, point):
        for c in range(CHUNKS):
            distance = point - c // 2
            if 1 <= distance < nr:
                chain_pass(ref, k, c, away == distance)

    def lane_arrive(ref, k):
        for c in range(CHUNKS):
            for d in range(1, ratio):
                other = ref.at[lax.rem(lane - d + ratio, ratio), spans[c]]
                remote(other, other, ln_send.at[k, c, d - 1], ln_recv.at[k, c, d - 1], (i, j)).wait_recv()

    def chain_end(ref, k):
        for c in range(CHUNKS):
            down, up = chain_copies(ref, k, c)

            @pl.when((pos <= i) & (pos > 0))
            def _():
                down.wait_send()

            @pl.when((pos >= i) & (pos < nr - 1))
            def _():
                up.wait_send()

            for copy in lane_copies(ref, k, c):
                copy.wait_send()

    partner = (i + 1 - 2 * core, j)
    mine_half = pl.ds(pl.multiple_of(core * half, half), half)
    other_half = pl.ds(pl.multiple_of((1 - core) * half, half), half)

    def reduce_a(k):
        return remote(part.at[k, other_half], half_in.at[k], red_send.at[k, 0], red_recv.at[k, 0], partner)

    def reduce_b(k):
        out = []
        for d in range(1, ny):
            to = lax.rem(yy + d, ny) * 2 + core
            out.append(
                remote(half_sum.at[k], half_y.at[k, yy], red_send.at[k, 1 + d],
                       red_recv.at[k, 1 + d], (to, j))
            )
        return out

    def reduce_c(k, out):
        return remote(out.at[mine_half], out.at[mine_half], red_send.at[k, 1], red_recv.at[k, 1], partner)

    def reduce_1(k):
        reduce_a(k).start()

    def reduce_2(k):
        reduce_a(k).wait_recv()
        half_sum[k] = part[k, mine_half] + half_in[k]
        for c in reduce_b(k):
            c.start()

    def reduce_3(k, out):
        for d in range(1, ny):
            slot = half_y.at[k, lax.rem(yy - d + ny, ny)]
            remote(slot, slot, red_send.at[k, 1 + d], red_recv.at[k, 1 + d], (i, j)).wait_recv()
        total = None
        for y in range(ny):
            term = jnp.where(yy == y, half_sum[k], half_y[k, y])
            total = term if total is None else total + term
        out[mine_half] = total
        reduce_c(k, out).start()

    def reduce_4(k, out):
        arrived = out.at[other_half]
        remote(arrived, arrived, red_send.at[k, 1], red_recv.at[k, 1], partner).wait_recv()

    def reduce_end(k, out):
        reduce_a(k).wait_send()
        for c in reduce_b(k):
            c.wait_send()
        reduce_c(k, out).wait_send()

    for y in range(ny):
        @pl.when(yy == y)
        def _():
            for k in range(3):
                half_y[k, y] = jnp.zeros((half, width), F32)

    @pl.when(i == 0)
    def _():
        pf[0] = a_ref[:width] * jnp.where(j == 0, 0.0, 1.0)
        pf[1] = a_ref[width:2 * width]

    def column_step(k, c):
        block = pf.at[k, spans[c]]
        column_arrive(block, pf_send.at[k, c], pf_recv.at[k, c])
        column_send(block, pf_send.at[k, c], pf_recv.at[k, c])

    p_rows, f_rows = pi.at[0], pi.at[1]
    for c in range(CHUNKS + 1):
        if c < CHUNKS:
            column_step(0, c)
            chain_source(p_rows, 0, c, pf.at[0])
        if c >= 1:
            chain_pass(p_rows, 0, c - 1, away > 0)
    for c in range(CHUNKS):
        column_step(1, c)
    lane_arrive(p_rows, 0)

    total = None
    for b in range(ratio):
        term = mm(pi[0, b], pi[0, b], NT)
        total = term if total is None else total + term
    part[0] = total
    reduce_1(0)
    total = None
    for b in range(ratio):
        term = mm(pi[0, b], a_ref[b * width:(b + 1) * width])
        total = term if total is None else total + term
    part[1] = total
    reduce_1(1)
    for c in range(CHUNKS):
        chain_source(f_rows, 1, c, pf.at[1])
    reduce_2(0)
    reduce_2(1)
    reduce_3(0, gram)
    reduce_3(1, zj)
    reduce_4(1, zj)
    for c in range(CHUNKS):
        chain_source(zi, 2, c, zj)

    @pl.when(i == 0)
    def _():
        first[...] = pi[0, 1]
        column_send(first, top_send, top_recv.at[0])

    chain_point(f_rows, 1, 1)
    chain_point(f_rows, 1, 2)
    reduce_4(0, gram)

    one = unit(width)
    aug[:, :width] = gram[...]
    aug[:, width:] = one
    steps = width // BLOCK
    last = nr - 1 + (CHUNKS - 1) // 2
    for q in range(steps):
        here = slice(q * BLOCK, (q + 1) * BLOCK)
        line = mm(small_factor(aug[here, here]), aug[here, :])
        low[here, :] = line[:, width:]
        if q + 1 < steps:
            below = slice((q + 1) * BLOCK, width)
            aug[below, :] = aug[below, :] - mm(line[:, below], line, TN)
        if q + 3 <= last:
            chain_point(f_rows, 1, q + 3)
        if q + 1 <= last:
            chain_point(zi, 2, q + 1)
    for point in range(steps + 1, last + 1):
        if point + 2 <= last:
            chain_point(f_rows, 1, point + 2)
        chain_point(zi, 2, point)

    column_arrive(first, top_send, top_recv.at[0])

    @pl.when(i > 0)
    def _():
        column_send(first, top_send, top_recv.at[0])

    for b in range(ratio):
        ri[b] = mm(low[...], pi[0, b]) + one * jnp.where(i * ratio + b == 1, 1.0, 0.0)
    lane_arrive(f_rows, 1)
    lane_arrive(zi, 2)
    total = None
    for b in range(ratio):
        xi[b] = mm(low[...], zi[b]) + pi[1, b]
        term = mm(ri[b], xi[b], NT)
        total = term if total is None else total + term
    part[2] = total
    reduce_1(2)
    reduce_2(2)
    reduce_3(2, ymat)
    reduce_4(2, ymat)
    for k, out in enumerate((gram, zj, ymat)):
        reduce_end(k, out)
    for k in range(2):
        for c in range(CHUNKS):
            column_end(pf.at[k, spans[c]], pf_send.at[k, c], pf_recv.at[k, c])
    for k, ref in enumerate((p_rows, f_rows, zi)):
        chain_end(ref, k)
    column_end(first, top_send, top_recv.at[0])


def small_factor(block):
    size = block.shape[0]
    step = 8
    eye = unit(size)
    act = jnp.concatenate([block, eye], axis=1)
    lanes = 2 * size
    done = []
    for q in range(size // step):
        count = size - q * step
        rows_id = lax.broadcasted_iota(jnp.int32, (count, lanes), 0)
        cols = [
            jnp.broadcast_to(act[:, q * step + t:q * step + t + 1], (count, lanes)) for t in range(step)
        ]
        top = act[:step]
        pivots = jnp.zeros((step, lanes), F32)
        saved = []
        for t in range(step):
            pivot = cols[t][t:t + 1]
            inv = 1.0 / pivot
            mult = jnp.where(rows_id > t, cols[t], 0.0) * inv
            for u in range(t + 1, step):
                cols[u] = cols[u] - mult * cols[u][t:t + 1]
            row = top[t:t + 1]
            top = top - mult[:step] * row
            pivots = jnp.where(rows_id[:step] == t, pivot, pivots)
            saved.append((mult, row))
        done.append(top / jnp.sqrt(pivots))
        if count > step:
            rest = act[step:]
            for mult, row in saved:
                rest = rest - mult[step:] * row
            act = rest
    return jnp.concatenate(done, axis=0)[:, size:]


def update_kernel(place, a_ref, pf, zj, low, first, ri, xi, ymat, out_ref, tt_ref, mid_ref):
    rows, width = a_ref.shape
    ratio = rows // width
    j = place[0]
    one = unit(width)
    w = low[...]
    err = 0.5 * (one - mm(w, first[...]))

    def more(state):
        k, acc, e = state
        return (k < 40) & (jnp.max(jnp.abs(e)) > 1e-10)

    def body(state):
        k, acc, e = state
        return k + 1, acc + mm(acc, e), mm(e, e)

    _, acc, _ = lax.while_loop(more, body, (0, one + err, mm(err, err)))
    tt_ref[...] = 0.5 * acc
    mid_ref[...] = mm(tt_ref[...], ymat[...])
    mid_ref[...] = 0.5 * mm(mid_ref[...], tt_ref[...], NT)

    def sides(r, x):
        return mm(tt_ref[...], x) - mm(mid_ref[...], r)

    r_cols = mm(w, pf[0]) + one * jnp.where(j == 1, 1.0, 0.0)
    w_cols = sides(r_cols, mm(w, zj[...]) + pf[1])
    for b in range(ratio):
        w_rows = sides(ri[b], xi[b])
        here = slice(b * width, (b + 1) * width)
        out_ref[here] = a_ref[here] - mm(w_rows, r_cols, TN) - mm(ri[b], w_cols, TN)


def solution(mesh):
    nr, nc = mesh.shape["row"], mesh.shape["col"]

    def step(matrix):
        rows, width = matrix.shape
        ratio = rows // width
        ny = nr // 2
        half = width // 2
        square = (width, width)
        vmem = pl.BlockSpec(memory_space=pltpu.VMEM)
        blocks = (ratio,) + square
        shapes = [(2,) + square, square, square, square, blocks, blocks, square]
        dma = pltpu.SemaphoreType.DMA
        parts = pl.pallas_call(
            functools.partial(gather_kernel, nr, nc),
            out_shape=[jax.ShapeDtypeStruct(s, F32) for s in shapes],
            in_specs=[vmem],
            out_specs=[vmem] * len(shapes),
            scratch_shapes=[
                pltpu.VMEM((2,) + blocks, F32),
                pltpu.VMEM(blocks, F32),
                pltpu.VMEM(square, F32),
                pltpu.VMEM((width, 2 * width), F32),
                pltpu.VMEM((3,) + square, F32),
                pltpu.VMEM((3, half, width), F32),
                pltpu.VMEM((3, half, width), F32),
                pltpu.VMEM((3, ny, half, width), F32),
                dma((3, ny + 1)), dma((3, ny + 1)),
                dma((2, CHUNKS, 2)), dma((2, CHUNKS)),
                dma((3, CHUNKS, 2)), dma((3, CHUNKS)),
                dma((3, CHUNKS, ratio - 1)), dma((3, CHUNKS, ratio - 1)),
                dma((2,)), dma((1,)),
            ],
            compiler_params=pltpu.CompilerParams(
                collective_id=0, has_side_effects=True, vmem_limit_bytes=48 * 2**20
            ),
            name="gather",
        )(matrix)
        return pl.pallas_call(
            update_kernel,
            out_shape=jax.ShapeDtypeStruct(matrix.shape, F32),
            in_specs=[pl.BlockSpec(memory_space=pltpu.SMEM)] + [vmem] * 8,
            out_specs=vmem,
            scratch_shapes=[pltpu.VMEM(square, F32), pltpu.VMEM(square, F32)],
            compiler_params=pltpu.CompilerParams(vmem_limit_bytes=48 * 2**20),
            name="update",
        )(lax.axis_index("col").reshape(1), matrix, *parts)

    return jax.shard_map(
        step, mesh=mesh, in_specs=(P("row", "col"),), out_specs=P("row", "col"), check_vma=False
    )
```

```python
import functools

import jax
import jax.numpy as jnp
from jax import lax
from jax.experimental import pallas as pl
from jax.experimental.pallas import tpu as pltpu
from jax.sharding import PartitionSpec as P

MESH = pl.DeviceIdType.MESH
F32 = jnp.float32
CHUNKS = 8
BLOCK = 64


def mm(left, right, dims=((1,), (0,))):
    return lax.dot_general(
        left, right, (dims, ((), ())), precision=lax.Precision.HIGHEST, preferred_element_type=F32
    )


def halves(x):
    high = x.astype(jnp.bfloat16)
    return high, (x - high.astype(F32)).astype(jnp.bfloat16)


def mm3(left, right, dims=((1,), (0,))):
    lh, ll = halves(left)
    rh, rl = halves(right)

    def dot(a, b):
        return lax.dot_general(a, b, (dims, ((), ())), preferred_element_type=F32)

    return dot(lh, rl) + dot(ll, rh) + dot(lh, rh)


NT = ((1,), (1,))
TN = ((0,), (0,))


def unit(size):
    same = lax.broadcasted_iota(jnp.int32, (size, size), 0) == lax.broadcasted_iota(jnp.int32, (size, size), 1)
    return jnp.where(same, 1.0, 0.0)


def doubling(acc, rest):
    e = rest[...]
    acc[...] = acc[...] + mm3(acc[...], e)
    rest[...] = mm3(e, e)


def gather_kernel(nr, nc, a_ref, acc, rest, rj, xj, ri, xi, ymat, *scratch):
    (pf, zj, low, first, pi, zi, gram, aug, part, half_in, half_sum, half_y, red_send, red_recv, pf_send, pf_recv, ch_send, ch_recv,
     ln_send, ln_recv, top_send, top_recv) = scratch
    rows, width = a_ref.shape
    ratio = rows // width
    half = width // 2
    ny = nr // 2
    i = lax.axis_index("row")
    j = lax.axis_index("col")
    lane = lax.rem(j, ratio)
    pos = j // ratio
    core = lax.rem(i, 2)
    yy = i // 2
    base = pos * ratio

    barrier = pltpu.get_barrier_semaphore()
    for d in range(1, nr):
        pl.semaphore_signal(barrier, 1, device_id=(lax.rem(i + d, nr), j), device_id_type=MESH)
    for d in range(1, ratio):
        pl.semaphore_signal(
            barrier, 1, device_id=(i, base + lax.rem(lane + d, ratio)), device_id_type=MESH
        )

    @pl.when(pos > 0)
    def _():
        pl.semaphore_signal(barrier, 1, device_id=(i, j - ratio), device_id_type=MESH)

    @pl.when(pos < nr - 1)
    def _():
        pl.semaphore_signal(barrier, 1, device_id=(i, j + ratio), device_id_type=MESH)

    pl.semaphore_wait(
        barrier,
        nr - 1 + ratio - 1 + jnp.where(pos > 0, 1, 0) + jnp.where(pos < nr - 1, 1, 0),
    )

    def remote(src, dst, send, recv, who):
        return pltpu.make_async_remote_copy(
            src_ref=src, dst_ref=dst, send_sem=send, recv_sem=recv, device_id=who,
            device_id_type=MESH,
        )

    chunk = width // CHUNKS
    spans = [pl.ds(c * chunk, chunk) for c in range(CHUNKS)]
    away = jnp.abs(pos - i)

    def column_copies(ref, sends, recv):
        return (
            remote(ref, ref, sends.at[0], recv, (jnp.minimum(i + 1, nr - 1), j)),
            remote(ref, ref, sends.at[1], recv, (jnp.minimum(i + 2, nr - 1), j)),
        )

    def column_arrive(ref, sends, recv):
        @pl.when(i > 0)
        def _():
            column_copies(ref, sends, recv)[0].wait_recv()

    def column_send(ref, sends, recv):
        @pl.when(core == 0)
        def _():
            to_odd, to_even = column_copies(ref, sends, recv)

            @pl.when(yy < ny - 1)
            def _():
                to_even.start()

            to_odd.start()

    def column_end(ref, sends, recv):
        @pl.when(core == 0)
        def _():
            to_odd, to_even = column_copies(ref, sends, recv)

            @pl.when(yy < ny - 1)
            def _():
                to_even.wait_send()

            to_odd.wait_send()

    def chain_copies(ref, k, c):
        mine = ref.at[lane, spans[c]]
        return (
            remote(mine, mine, ch_send.at[k, c, 0], ch_recv.at[k, c], (i, jnp.maximum(j - ratio, 0))),
            remote(mine, mine, ch_send.at[k, c, 1], ch_recv.at[k, c], (i, jnp.minimum(j + ratio, nc - 1))),
        )

    def lane_copies(ref, k, c):
        mine = ref.at[lane, spans[c]]
        return [
            remote(mine, mine, ln_send.at[k, c, d - 1], ln_recv.at[k, c, d - 1],
                   (i, base + lax.rem(lane + d, ratio)))
            for d in range(1, ratio)
        ]

    def chain_push(ref, k, c):
        down, up = chain_copies(ref, k, c)

        @pl.when((pos <= i) & (pos > 0))
        def _():
            down.start()

        @pl.when((pos >= i) & (pos < nr - 1))
        def _():
            up.start()

        for copy in lane_copies(ref, k, c):
            copy.start()

    def chain_source(ref, k, c, block):
        @pl.when(away == 0)
        def _():
            ref[lane, spans[c]] = block[spans[c]]
            chain_push(ref, k, c)

    def chain_pass(ref, k, c, far):
        @pl.when(far)
        def _():
            chain_copies(ref, k, c)[0].wait_recv()
            chain_push(ref, k, c)

    def chain_point(ref, k, point):
        for c in range(CHUNKS):
            distance = point - 2 * c // CHUNKS
            if 1 <= distance < nr:
                chain_pass(ref, k, c, away == distance)

    def lane_arrive(ref, k):
        for c in range(CHUNKS):
            for d in range(1, ratio):
                other = ref.at[lax.rem(lane - d + ratio, ratio), spans[c]]
                remote(other, other, ln_send.at[k, c, d - 1], ln_recv.at[k, c, d - 1], (i, j)).wait_recv()

    def chain_end(ref, k):
        for c in range(CHUNKS):
            down, up = chain_copies(ref, k, c)

            @pl.when((pos <= i) & (pos > 0))
            def _():
                down.wait_send()

            @pl.when((pos >= i) & (pos < nr - 1))
            def _():
                up.wait_send()

            for copy in lane_copies(ref, k, c):
                copy.wait_send()

    partner = (i + 1 - 2 * core, j)
    mine_half = pl.ds(pl.multiple_of(core * half, half), half)
    other_half = pl.ds(pl.multiple_of((1 - core) * half, half), half)

    def reduce_a(k):
        return remote(part.at[k, other_half], half_in.at[k], red_send.at[k, 0], red_recv.at[k, 0], partner)

    def reduce_b(k):
        out = []
        for d in range(1, ny):
            to = lax.rem(yy + d, ny) * 2 + core
            out.append(
                remote(half_sum.at[k], half_y.at[k, yy], red_send.at[k, 1 + d],
                       red_recv.at[k, 1 + d], (to, j))
            )
        return out

    def reduce_c(k, out):
        return remote(out.at[mine_half], out.at[mine_half], red_send.at[k, 1], red_recv.at[k, 1], partner)

    def reduce_1(k):
        reduce_a(k).start()

    def reduce_2(k):
        reduce_a(k).wait_recv()
        half_sum[k] = part[k, mine_half] + half_in[k]
        for c in reduce_b(k):
            c.start()

    def reduce_3(k, out):
        for d in range(1, ny):
            slot = half_y.at[k, lax.rem(yy - d + ny, ny)]
            remote(slot, slot, red_send.at[k, 1 + d], red_recv.at[k, 1 + d], (i, j)).wait_recv()
        total = None
        for y in range(ny):
            term = jnp.where(yy == y, half_sum[k], half_y[k, y])
            total = term if total is None else total + term
        out[mine_half] = total
        reduce_c(k, out).start()

    def reduce_4(k, out):
        arrived = out.at[other_half]
        remote(arrived, arrived, red_send.at[k, 1], red_recv.at[k, 1], partner).wait_recv()

    def reduce_end(k, out):
        reduce_a(k).wait_send()
        for c in reduce_b(k):
            c.wait_send()
        reduce_c(k, out).wait_send()

    for y in range(ny):
        @pl.when(yy == y)
        def _():
            for k in range(3):
                half_y[k, y] = jnp.zeros((half, width), F32)

    @pl.when(i == 0)
    def _():
        pf[0] = a_ref[:width] * jnp.where(j == 0, 0.0, 1.0)
        pf[1] = a_ref[width:2 * width]

    def column_step(k, c):
        block = pf.at[k, spans[c]]
        column_arrive(block, pf_send.at[k, c], pf_recv.at[k, c])
        column_send(block, pf_send.at[k, c], pf_recv.at[k, c])

    p_rows, f_rows = pi.at[0], pi.at[1]
    for c in range(CHUNKS + 1):
        if c < CHUNKS:
            column_step(0, c)
            chain_source(p_rows, 0, c, pf.at[0])
        if c >= 1:
            chain_pass(p_rows, 0, c - 1, away > 0)
    for c in range(CHUNKS):
        column_step(1, c)
    lane_arrive(p_rows, 0)

    total = None
    for b in range(ratio):
        term = mm3(pi[0, b], pi[0, b], NT)
        total = term if total is None else total + term
    part[0] = total
    reduce_1(0)
    total = None
    for b in range(ratio):
        term = mm3(pi[0, b], a_ref[b * width:(b + 1) * width])
        total = term if total is None else total + term
    part[1] = total
    reduce_1(1)
    for c in range(CHUNKS):
        chain_source(f_rows, 1, c, pf.at[1])
    reduce_2(0)
    reduce_2(1)
    reduce_3(0, gram)
    reduce_3(1, zj)
    reduce_4(1, zj)
    for c in range(CHUNKS):
        chain_source(zi, 2, c, zj)

    @pl.when(i == 0)
    def _():
        first[...] = pi[0, 1]
        column_send(first, top_send, top_recv.at[0])

    reduce_4(0, gram)
    chain_point(f_rows, 1, 1)

    one = unit(width)
    aug[:, :width] = gram[...]
    aug[:, width:] = one
    steps = width // BLOCK
    last = nr
    for q in range(steps):
        here = slice(q * BLOCK, (q + 1) * BLOCK)
        line = mm(small_factor(aug[here, here]), aug[here, :])
        low[here, :] = line[:, width:]
        if q + 1 < steps:
            below = slice((q + 1) * BLOCK, width)
            aug[below, :] = aug[below, :] - mm(line[:, below], line, TN)
        if q + 2 <= last:
            chain_point(f_rows, 1, q + 2)
        if q + 1 <= last:
            chain_point(zi, 2, q + 1)
    for point in range(steps + 1, last + 1):
        if point + 1 <= last:
            chain_point(f_rows, 1, point + 1)
        chain_point(zi, 2, point)

    column_arrive(first, top_send, top_recv.at[0])

    @pl.when(i > 0)
    def _():
        column_send(first, top_send, top_recv.at[0])

    for b in range(ratio):
        ri[b] = mm3(low[...], pi[0, b]) + one * jnp.where(i * ratio + b == 1, 1.0, 0.0)
    lane_arrive(f_rows, 1)
    lane_arrive(zi, 2)
    total = None
    for b in range(ratio):
        xi[b] = mm3(low[...], zi[b]) + pi[1, b]
        term = mm3(ri[b], xi[b], NT)
        total = term if total is None else total + term
    part[2] = total
    reduce_1(2)
    err = 0.5 * (one - mm3(low[...], first[...]))
    acc[...] = one + err
    rest[...] = mm3(err, err)
    doubling(acc, rest)
    reduce_2(2)
    doubling(acc, rest)
    doubling(acc, rest)
    rj[...] = mm3(low[...], pf[0]) + one * jnp.where(j == 1, 1.0, 0.0)
    xj[...] = mm3(low[...], zj[...]) + pf[1]
    reduce_3(2, ymat)
    doubling(acc, rest)
    reduce_4(2, ymat)
    for k, out in enumerate((gram, zj, ymat)):
        reduce_end(k, out)
    for k in range(2):
        for c in range(CHUNKS):
            column_end(pf.at[k, spans[c]], pf_send.at[k, c], pf_recv.at[k, c])
    for k, ref in enumerate((p_rows, f_rows, zi)):
        chain_end(ref, k)
    column_end(first, top_send, top_recv.at[0])


def small_factor(block):
    size = block.shape[0]
    step = 8
    eye = unit(size)
    act = jnp.concatenate([block, eye], axis=1)
    lanes = 2 * size
    done = []
    for q in range(size // step):
        count = size - q * step
        rows_id = lax.broadcasted_iota(jnp.int32, (count, lanes), 0)
        cols = [
            jnp.broadcast_to(act[:, q * step + t:q * step + t + 1], (count, lanes)) for t in range(step)
        ]
        top = act[:step]
        pivots = jnp.zeros((step, lanes), F32)
        saved = []
        for t in range(step):
            pivot = cols[t][t:t + 1]
            inv = 1.0 / pivot
            mult = jnp.where(rows_id > t, cols[t], 0.0) * inv
            for u in range(t + 1, step):
                cols[u] = cols[u] - mult * cols[u][t:t + 1]
            row = top[t:t + 1]
            top = top - mult[:step] * row
            pivots = jnp.where(rows_id[:step] == t, pivot, pivots)
            saved.append((mult, row))
        done.append(top / jnp.sqrt(pivots))
        if count > step:
            rest = act[step:]
            for mult, row in saved:
                rest = rest - mult[step:] * row
            act = rest
    return jnp.concatenate(done, axis=0)[:, size:]


def update_kernel(a_ref, acc, rest, rj, xj, ri, xi, ymat, out_ref, tt_ref, mid_ref, rest_ref):
    rows, width = a_ref.shape
    ratio = rows // width
    tt_ref[...] = acc[...]
    rest_ref[...] = rest[...]

    def more(state):
        k, size = state
        return (k < 40) & (size > 1e-10)

    def body(state):
        doubling(tt_ref, rest_ref)
        return state[0] + 1, jnp.max(jnp.abs(rest_ref[...]))

    lax.while_loop(more, body, (0, jnp.max(jnp.abs(rest_ref[...]))))
    tt_ref[...] = 0.5 * tt_ref[...]
    mid_ref[...] = mm3(tt_ref[...], ymat[...])
    mid_ref[...] = 0.5 * mm3(mid_ref[...], tt_ref[...], NT)

    def sides(r, x):
        return mm3(tt_ref[...], x) - mm3(mid_ref[...], r)

    w_cols = sides(rj[...], xj[...])
    for b in range(ratio):
        w_rows = sides(ri[b], xi[b])
        here = slice(b * width, (b + 1) * width)
        out_ref[here] = a_ref[here] - mm3(w_rows, rj[...], TN) - mm3(ri[b], w_cols, TN)


def solution(mesh):
    nr, nc = mesh.shape["row"], mesh.shape["col"]

    def step(matrix):
        rows, width = matrix.shape
        ratio = rows // width
        ny = nr // 2
        half = width // 2
        square = (width, width)
        vmem = pl.BlockSpec(memory_space=pltpu.VMEM)
        blocks = (ratio,) + square
        shapes = [square, square, square, square, blocks, blocks, square]
        dma = pltpu.SemaphoreType.DMA
        parts = pl.pallas_call(
            functools.partial(gather_kernel, nr, nc),
            out_shape=[jax.ShapeDtypeStruct(s, F32) for s in shapes],
            in_specs=[vmem],
            out_specs=[vmem] * len(shapes),
            scratch_shapes=[
                pltpu.VMEM((2,) + square, F32),
                pltpu.VMEM(square, F32),
                pltpu.VMEM(square, F32),
                pltpu.VMEM(square, F32),
                pltpu.VMEM((2,) + blocks, F32),
                pltpu.VMEM(blocks, F32),
                pltpu.VMEM(square, F32),
                pltpu.VMEM((width, 2 * width), F32),
                pltpu.VMEM((3,) + square, F32),
                pltpu.VMEM((3, half, width), F32),
                pltpu.VMEM((3, half, width), F32),
                pltpu.VMEM((3, ny, half, width), F32),
                dma((3, ny + 1)), dma((3, ny + 1)),
                dma((2, CHUNKS, 2)), dma((2, CHUNKS)),
                dma((3, CHUNKS, 2)), dma((3, CHUNKS)),
                dma((3, CHUNKS, ratio - 1)), dma((3, CHUNKS, ratio - 1)),
                dma((2,)), dma((1,)),
            ],
            compiler_params=pltpu.CompilerParams(
                collective_id=0, has_side_effects=True, vmem_limit_bytes=48 * 2**20
            ),
            name="gather",
        )(matrix)
        return pl.pallas_call(
            update_kernel,
            out_shape=jax.ShapeDtypeStruct(matrix.shape, F32),
            in_specs=[vmem] * 8,
            out_specs=vmem,
            scratch_shapes=[pltpu.VMEM(square, F32)] * 3,
            compiler_params=pltpu.CompilerParams(vmem_limit_bytes=48 * 2**20),
            name="update",
        )(matrix, *parts)

    return jax.shard_map(
        step, mesh=mesh, in_specs=(P("row", "col"),), out_specs=P("row", "col"), check_vma=False
    )
```
